32 devices in a mesh: gx: 8 (over z, y), gy: 4 (over x, core).
Axes of the slice: x: 2, y: 2, z: 4, core: 2. Of those that a mesh axis runs over, the one named last changes fastest.
Arguments:
- ocean_current: float32 [2, 256, 2048], P(None, 'gx', 'gy'), may hold values from -6 to 6
- floe_state: float32 [1024, 4, 128], P(('gx', 'gy')), may hold values from -6 to 6
- floe_source: int32 [1024, 1], P(('gx', 'gy')), may hold values from 0 to 31; in each aligned block of 32 rows (0 to 31, 32 to 63, ...) at most 2 rows name the same one
- floe_patch: int32 [1024, 1], P(('gx', 'gy')), may hold values from 0 to 63
- floe_cell: int32 [1024, 2, 128], P(('gx', 'gy')), may hold values from 0 to 14
- floe_frac: float32 [1024, 2, 128], P(('gx', 'gy')), may hold values from 0 to 1
- bond_blocks: int32 [1024, 2, 4], P(('gx', 'gy')), may hold values from 0 to 31, as said below
- bond_lanes: int32 [1024, 4, 128], P(('gx', 'gy')), may hold values from 0 to 127
- bond_stiff: float32 [1024, 4, 128], P(('gx', 'gy')), may hold values from 0.5 to 2
- contact_blocks: int32 [1024, 2, 4], P(('gx', 'gy')), may hold values from 0 to 31, as said below
- contact_lanes: int32 [1024, 4, 128], P(('gx', 'gy')), may hold values from 0 to 127
Outputs:
- floe_final: float32 [1024, 4, 128], P(('gx', 'gy'))
- ocean_stress: float32 [2, 256, 2048], P(None, 'gx', 'gy')
The draws below stay inside these ranges and needn't reach their ends.
Inputs may be any that keep to these rules, and one draw needn't show every extreme that they name: `floe_source`: the blocks of one region name one tile at most 2 times; in every region some tile is named exactly 2 times. bond_blocks[k, 0, s] is a region code 0 to 4; bond_blocks[k, 1, s] is below 32 where the code is 0, else below 16. contact_blocks[k, 0, s] is a region code 0 to 4; contact_blocks[k, 1, s] is below 32 where the code is 0, else below 16.
All inputs are finite; a program needn't handle non-finite values.
Results may differ from the reference program's by a relative error of at most 0.00012.
Values sent between devices are 32-bit elements; how exact they have to be, the bound alone decides.
A program may use at most 64 MiB of HBM per device.

```python
import math
import jax
import jax.numpy as jnp
import numpy as np
from jax import lax

LANES = 128
PS = 16
EDGE = 16
NB = 4
NC = 4
SUBSTEPS = 4
BLOCKS_DEV = 32
TILE_X = 32
TILE_Y = 512
NS = 8
GRID_X = 256
GRID_Y = 2048
NBLK = 1024
PATCHES = 64
CAP = 2
N_GX = 8
N_GY = 4


def partner_draw(key, slots):
    key_region, key_near, key_rim = jax.random.split(key, 3)
    region = jax.random.randint(key_region, (NBLK, slots), 0, 5, dtype=jnp.int32)
    near = jax.random.randint(key_near, (NBLK, slots), 0, BLOCKS_DEV, dtype=jnp.int32)
    rim = jax.random.randint(key_rim, (NBLK, slots), 0, EDGE, dtype=jnp.int32)
    region = region.at[0, 0].set(0).at[0, 1].set(4)
    near = near.at[0, 0].set(BLOCKS_DEV - 1)
    number = jnp.where(region == 0, near, rim)
    return jnp.stack([region, number], axis=1)


def draw_bond_blocks(key, part):
    key = jax.random.fold_in(key, 11)
    return partner_draw(key, NB)


def draw_contact_blocks(key, part):
    key = jax.random.fold_in(key, 23)
    return partner_draw(key, NC)


def touch_ends(array, stream_key, smallest, high):
    dims = array.shape
    place = [jax.random.randint(jax.random.fold_in(stream_key, axis), (), 0, dims[axis]) for axis in range(len(dims))]
    array = array.at[tuple(place)].set(smallest)
    longest = dims.index(max(dims))
    place[longest] = (place[longest] + 1) % dims[longest]
    return array.at[tuple(place)].set(high)


def level_of(stream_key, shape, cuts, least, largest):
    factor_of = 1.0
    for axis_at, blocks in cuts:
        heights = jax.random.uniform(jax.random.fold_in(jax.random.fold_in(stream_key, 6), axis_at), (blocks,), jnp.float32, least / len(cuts), largest / len(cuts))
        factor_of = factor_of * jnp.repeat(jnp.exp(heights), shape[axis_at] // blocks).reshape((-1,) + (1,) * (len(shape) - 1 - axis_at))
    return factor_of


def deal_out(rng, own, number, rows, amount, top, bound, slope):
    ranking = jax.random.permutation(rng, amount)
    heavy_load, ordinary = load_shares(amount, rows * top, bound, slope, True), load_shares(amount, rows * top, bound, slope, False)
    places = jnp.arange(amount)

    def named(lengths, rotation):
        used = int((lengths > 0).sum())
        fixed = max(1, used // 4)
        shifted = fixed + (places - fixed + rotation * (used - fixed)) % max(1, amount - fixed)
        return jnp.zeros((amount,), jnp.int32).at[ranking[jnp.where(places < fixed, places, shifted)]].set(jnp.asarray(lengths, jnp.int32))

    lengths = jnp.where(number % 4 == 0, named(heavy_load, number // 4), named(ordinary, number - number // 4 - 1))
    mixed = jax.random.permutation(jax.random.fold_in(own, 3), amount)
    donor, taker = mixed[0:amount // 2 * 2:2], mixed[1:amount // 2 * 2:2]
    margin = jnp.minimum(lengths[donor] - 1, bound - lengths[taker]) // 2
    margin = jnp.where((donor == ranking[0]) | (taker == ranking[0]) | (lengths[taker] == 0), 0, jnp.maximum(margin, 0))
    shifted = jax.random.randint(jax.random.fold_in(own, 4), (amount // 2,), 0, 1 << 20) % (margin + 1)
    lengths = lengths.at[donor].add(-shifted).at[taker].add(shifted)
    members = jnp.searchsorted(jnp.cumsum(lengths), jnp.arange(rows * top), side="right").astype(jnp.int32)
    table = members.reshape(top, rows).T
    table = table[jax.random.permutation(jax.random.fold_in(own, 1), rows)]
    rotation = jax.random.randint(jax.random.fold_in(own, 2), (rows, 1), 0, top)
    return jnp.take_along_axis(table, (jnp.arange(top)[None, :] + rotation) % top, axis=1)


def load_shares(number_of, total, limit, lean, full):
    portions = [(1 << 20) // math.isqrt(grade ** lean) + 1 for grade in range(1, number_of + 1)]
    largest = limit if full else min(limit, max(-(-total // number_of), total * portions[0] // sum(portions)))
    least = 1 if total - largest >= number_of - 1 else 0
    counts, rest = [largest] + [least] * (number_of - 1), total - largest - least * (number_of - 1)
    while rest > 0:
        movable = [i for i in range(1, number_of) if counts[i] < largest] or [i for i in range(1, number_of) if counts[i] < limit]
        whole, left = sum([portions[i] for i in movable]), rest
        for i in movable:
            addition = min(limit - counts[i], max(1, left * portions[i] // whole), rest)
            counts[i] = counts[i] + addition
            rest = rest - addition
    return np.array(counts)


def noise(own_key, shape, deviation, limit, cuts=(), held_as=jnp.bfloat16):
    level = level_of(own_key, shape, cuts, -0.22, 0.18) if cuts else 1.0
    values = jax.random.normal(own_key, shape, jnp.float32) * deviation * level
    return jnp.minimum(jnp.maximum(values, -limit), limit).astype(held_as)


def setup_inputs(seed: int = 0) -> dict:
    key_of = jax.random.split(jax.random.key(seed), 12)
    ocean_current = noise(key_of[0], (2, GRID_X, GRID_Y), 1.0, 6.0, ((1, 8), (2, 4)), jnp.float32)
    floe_state = noise(key_of[1], (NBLK, 4, LANES), 1.0, 6.0, ((0, 32),), jnp.float32)
    floe_source_keys = jax.random.split(jax.random.fold_in(key_of[2], 1), NBLK // BLOCKS_DEV)
    floe_source_turns = jax.random.permutation(jax.random.fold_in(key_of[2], 3), NBLK // BLOCKS_DEV)
    floe_source = jax.vmap(lambda own, number: deal_out(jax.random.fold_in(key_of[2], 2), own, number, BLOCKS_DEV, N_GX * N_GY, 1, CAP, 2))(floe_source_keys, floe_source_turns).reshape((NBLK, 1))
    floe_patch = touch_ends(jax.random.randint(key_of[3], (NBLK, 1), 0, PATCHES), jax.random.fold_in(key_of[3], 1), 0, PATCHES - 1).astype(jnp.int32)
    floe_cell = touch_ends(jax.random.randint(key_of[4], (NBLK, 2, LANES), 0, PS - 1), jax.random.fold_in(key_of[4], 1), 0, (PS - 1) - 1).astype(jnp.int32)
    floe_frac = jnp.clip(1.0 * jax.random.uniform(key_of[5], (NBLK, 2, LANES), jnp.float32) ** level_of(key_of[5], (NBLK, 2, LANES), ((0, 32),), -0.2, 0.2), 0.0, 1.0)
    bond_blocks = draw_bond_blocks(jax.random.fold_in(key_of[11], 71), 0)
    bond_lanes = touch_ends(jax.random.randint(key_of[7], (NBLK, NB, LANES), 0, LANES), jax.random.fold_in(key_of[7], 1), 0, LANES - 1).astype(jnp.int32)
    bond_stiff = jnp.clip(jnp.exp(math.log(2.0) - 1.3862944 * jax.random.uniform(key_of[8], (NBLK, NB, LANES), jnp.float32) ** level_of(key_of[8], (NBLK, NB, LANES), ((0, 32),), -0.2, 0.2)), 0.5, 2.0)
    contact_blocks = draw_contact_blocks(jax.random.fold_in(key_of[11], 71), 0)
    contact_lanes = touch_ends(jax.random.randint(key_of[10], (NBLK, NC, LANES), 0, LANES), jax.random.fold_in(key_of[10], 1), 0, LANES - 1).astype(jnp.int32)
    return dict(ocean_current=ocean_current, floe_state=floe_state, floe_source=floe_source, floe_patch=floe_patch, floe_cell=floe_cell, floe_frac=floe_frac, bond_blocks=bond_blocks, bond_lanes=bond_lanes, bond_stiff=bond_stiff, contact_blocks=contact_blocks, contact_lanes=contact_lanes)


HIGH = lax.Precision.HIGHEST

def weights(cell, frac):
    ticks = jnp.arange(PS, dtype=jnp.int32)[None, :, None]
    col_i = cell[:, 0, None, :]
    row_j = cell[:, 1, None, :]
    frac_x = frac[:, 0, None, :]
    frac_y = frac[:, 1, None, :]
    col_weight = (1.0 - frac_x) * (ticks == col_i) + frac_x * (ticks == col_i + 1)
    row_weight = (1.0 - frac_y) * (ticks == row_j) + frac_y * (ticks == row_j + 1)
    return (col_weight.astype(jnp.float32), row_weight.astype(jnp.float32))

def sample(patch, col_weight, row_weight):
    values = patch.reshape(patch.shape[0], 2, PS, PS)
    inner = jnp.einsum('kcab,kbf->kcaf', values, row_weight, precision=HIGH)
    return lax.optimization_barrier(jnp.sum(col_weight[:, None] * inner, axis=2))

def deposit(stress, col_weight, row_weight):
    spread = col_weight[:, None] * stress[:, :, None, :]
    result = jnp.einsum('kcaf,kbf->kcab', spread, row_weight, precision=HIGH)
    return result.reshape(stress.shape[0], 2, PS * PS)

def pick_lanes(partner_blocks, lanes):
    index = jnp.broadcast_to(lanes[:, :, None, :], partner_blocks.shape)
    return jnp.take_along_axis(partner_blocks, index, axis=3)

def interact(own, partner, stiff, current):
    dx = partner[:, :, 0] - own[:, None, 0]
    dy = partner[:, :, 1] - own[:, None, 1]
    du = partner[:, :, 2] - own[:, None, 2]
    dv = partner[:, :, 3] - own[:, None, 3]
    bond_x = lax.optimization_barrier(jnp.sum(stiff * dx[:, :NB] + 0.2 * du[:, :NB], axis=1))
    bond_y = lax.optimization_barrier(jnp.sum(stiff * dy[:, :NB] + 0.2 * dv[:, :NB], axis=1))
    near_x = dx[:, NB:]
    near_y = dy[:, NB:]
    dist = jnp.sqrt(near_x * near_x + near_y * near_y)
    push = 2.0 * jnp.maximum(1.5 - dist, 0.0) / jnp.maximum(dist, 0.5)
    touch_x = -lax.optimization_barrier(jnp.sum(push * near_x, axis=1))
    touch_y = -lax.optimization_barrier(jnp.sum(push * near_y, axis=1))
    slip_x = current[:, 0] - own[:, 2]
    slip_y = current[:, 1] - own[:, 3]
    speed = jnp.sqrt(slip_x * slip_x + slip_y * slip_y)
    drag_x = 0.5 * speed * slip_x
    drag_y = 0.5 * speed * slip_y
    new_u = own[:, 2] + 0.05 * (bond_x + touch_x + drag_x)
    new_v = own[:, 3] + 0.05 * (bond_y + touch_y + drag_y)
    new_x = own[:, 0] + 0.05 * new_u
    new_y = own[:, 1] + 0.05 * new_v
    return (jnp.stack([new_x, new_y, new_u, new_v], axis=1), jnp.stack([drag_x, drag_y], axis=1))

def reference(ocean_current, floe_state, floe_source, floe_patch, floe_cell, floe_frac, bond_blocks, bond_lanes, bond_stiff, contact_blocks, contact_lanes):
    devices = N_GX * N_GY
    npx = TILE_X // PS
    npy = TILE_Y // PS
    patches = ocean_current.reshape(2, N_GX, npx, PS, N_GY, npy, PS).transpose(1, 4, 2, 5, 0, 3, 6).reshape(devices * PATCHES, 2, PS * PS)
    global_patch = (floe_source[:, 0] * PATCHES + floe_patch[:, 0]).astype(jnp.int32)
    mine = patches[global_patch]
    col_weight, row_weight = weights(floe_cell, floe_frac)

    def sample_one(items):
        return sample(items[0], items[1], items[2])
    current = lax.map(sample_one, (mine.reshape(devices, BLOCKS_DEV, 2, PS * PS), col_weight.reshape(devices, BLOCKS_DEV, PS, LANES), row_weight.reshape(devices, BLOCKS_DEV, PS, LANES)))
    current = current.reshape(NBLK, 2, LANES)
    region = jnp.concatenate([bond_blocks[:, 0], contact_blocks[:, 0]], axis=1)
    number = jnp.concatenate([bond_blocks[:, 1], contact_blocks[:, 1]], axis=1)
    owner = (jnp.arange(NBLK, dtype=jnp.int32) // BLOCKS_DEV)[:, None]
    col_a = owner // N_GY
    row_b = owner % N_GY
    dev_one = (col_a - 1) % N_GX * N_GY + row_b
    dev_two = (col_a + 1) % N_GX * N_GY + row_b
    dev_three = col_a * N_GY + (row_b - 1) % N_GY
    dev_four = col_a * N_GY + (row_b + 1) % N_GY
    far_end = BLOCKS_DEV - EDGE + number
    partner_block = jnp.where(region == 0, owner * BLOCKS_DEV + number, jnp.where(region == 1, dev_one * BLOCKS_DEV + far_end, jnp.where(region == 2, dev_two * BLOCKS_DEV + number, jnp.where(region == 3, dev_three * BLOCKS_DEV + far_end, dev_four * BLOCKS_DEV + number)))).astype(jnp.int32)
    lanes = jnp.concatenate([bond_lanes, contact_lanes], axis=1)
    state = floe_state
    drag_total = jnp.zeros((NBLK, 2, LANES), jnp.float32)
    for step in range(SUBSTEPS):

        def advance(items):
            own, index, lane, stiff, flow = items
            partner = pick_lanes(state[index], lane)
            return interact(own, partner, stiff, flow)
        state_new, drag = lax.map(advance, (state.reshape(devices, BLOCKS_DEV, 4, LANES), partner_block.reshape(devices, BLOCKS_DEV, NS), lanes.reshape(devices, BLOCKS_DEV, NS, LANES), bond_stiff.reshape(devices, BLOCKS_DEV, NB, LANES), current.reshape(devices, BLOCKS_DEV, 2, LANES)))
        state = state_new.reshape(NBLK, 4, LANES)
        drag_total = drag_total + drag.reshape(NBLK, 2, LANES)
    floe_stress = -drag_total / SUBSTEPS

    def deposit_one(items):
        return deposit(items[0], items[1], items[2])
    pieces = lax.map(deposit_one, (floe_stress.reshape(devices, BLOCKS_DEV, 2, LANES), col_weight.reshape(devices, BLOCKS_DEV, PS, LANES), row_weight.reshape(devices, BLOCKS_DEV, PS, LANES)))
    pieces = pieces.reshape(NBLK, 2, PS * PS)
    summed = jax.ops.segment_sum(pieces, global_patch, num_segments=devices * PATCHES)
    ocean_stress = summed.reshape(N_GX, N_GY, npx, npy, 2, PS, PS).transpose(4, 0, 2, 5, 1, 3, 6).reshape(2, GRID_X, GRID_Y)
    return (state, ocean_stress)
```

```python
import functools
import jax
import jax.numpy as jnp
from jax import lax
from jax.experimental import pallas as pl
from jax.experimental.pallas import tpu as pltpu
from jax.sharding import PartitionSpec as P

PS = 16
EDGE = 16
NB = 4
NC = 4
NS = NB + NC
SUBSTEPS = 4
LANES = 128
PAD = 8
MESH = pl.DeviceIdType.MESH
F32 = jnp.float32
BF16 = jnp.bfloat16


def iota(shape, dim):
    return lax.broadcasted_iota(jnp.int32, shape, dim)


def split_bf16(value, parts):
    out = []
    for _ in range(parts):
        piece = value.astype(BF16)
        out.append(piece)
        value = value - piece.astype(F32)
    return out


def one_hot_dot(picks, values, parts):
    left = picks.astype(BF16)
    left = jnp.concatenate([left] * parts, axis=1)
    right = jnp.concatenate(split_bf16(values, parts), axis=0)
    return jnp.dot(left, right, preferred_element_type=F32)


def half_bit(shape):
    return (iota(shape, 1) // 32) % 2


def swap_halves(value):
    ahead = pltpu.roll(value, LANES - 32, 1)
    behind = pltpu.roll(value, 32, 1)
    return jnp.where(half_bit(value.shape) == 0, ahead, behind)


def to_row(column, count):
    eye = iota((count, count), 0) == iota((count, count), 1)
    return jnp.sum(jnp.where(eye, column, 0), axis=0, keepdims=True)


def kernel(
    cols,
    rows,
    blocks,
    row_of,
    source_of,
    ocean,
    state_in,
    code_row,
    source_col,
    cell,
    frac,
    bond_lanes,
    stiff_in,
    contact_lanes,
    state_out,
    stress_out,
    pool0,
    pool1,
    pool2,
    pool3,
    codes,
    outgoing,
    incoming,
    returned,
    arrived,
    turned,
    bond_index,
    contact_index,
    bond_got,
    contact_got,
    row_w,
    col_w,
    row_split,
    current,
    rank_b,
    pieces,
    stress,
    halo_send,
    halo_recv,
    all_send,
    all_recv,
):
    pools = (pool0, pool1, pool2, pool3)
    devices = cols * rows
    ax = lax.axis_index("gx")
    by = lax.axis_index("gy")
    me = ax * rows + by
    npy = ocean.shape[2] // PS

    def place_of(number):
        return (number // rows, lax.rem(number, rows))

    barrier = pltpu.get_barrier_semaphore()

    @pl.loop(1, devices)
    def _(i):
        pl.semaphore_signal(
            barrier, inc=1, device_id=place_of(lax.rem(me + i, devices)), device_id_type=MESH
        )

    codes[pl.ds(me, 1)] = code_row[...].reshape(1, 1, LANES)
    pool0[pl.ds(PAD, 4 * blocks), :] = state_in[...]
    for pool in pools:
        pool[pl.ds(0, PAD), :] = jnp.zeros((PAD, LANES), F32)
        pool[pl.ds(PAD + 4 * (blocks + 4 * EDGE), PAD), :] = jnp.zeros((PAD, LANES), F32)
    pl.semaphore_wait(barrier, devices - 1)

    def all_copy(source, target, which, number):
        return pltpu.make_async_remote_copy(
            src_ref=source,
            dst_ref=target,
            send_sem=all_send.at[which],
            recv_sem=all_recv.at[which],
            device_id=place_of(number),
            device_id_type=MESH,
        )

    other = lax.rem(me + 1, devices)

    @pl.loop(1, devices)
    def _(i):
        to = lax.rem(me + i, devices)
        all_copy(codes.at[pl.ds(me, 1)], codes.at[pl.ds(me, 1)], 0, to).start()

    def all_codes():
        part = codes.at[pl.ds(0, devices - 1)]
        return all_copy(part, part, 0, other)

    def all_blocks(outs, ins, which):
        size = 8 * (devices - 1)
        return all_copy(outs.at[pl.ds(0, size), :], outs.at[pl.ds(0, size), :], which, other)

    def send_blocks(outs, ins, which):
        mine = pl.ds(pl.multiple_of(me * 8, 8), 8)
        land = ins.at[me] if which == 1 else ins.at[mine, :]

        @pl.loop(1, devices)
        def _(i):
            to = lax.rem(me + i, devices)
            part = outs.at[pl.ds(pl.multiple_of(to * 8, 8), 8), :]
            all_copy(part, land, which, to).start()

        land[...] = outs[mine, :]

    last = PAD + 4 * (blocks - EDGE)
    targets = (
        (last, (lax.rem(ax + 1, cols), by)),
        (PAD, (lax.rem(ax + cols - 1, cols), by)),
        (last, (ax, lax.rem(by + 1, rows))),
        (PAD, (ax, lax.rem(by + rows - 1, rows))),
    )

    def halo(step):
        pool = pools[step]
        out = []
        for side, (start, device) in enumerate(targets):
            out.append(
                pltpu.make_async_remote_copy(
                    src_ref=pool.at[pl.ds(start, 4 * EDGE), :],
                    dst_ref=pool.at[pl.ds(PAD + 4 * (blocks + side * EDGE), 4 * EDGE), :],
                    send_sem=halo_send.at[step, side],
                    recv_sem=halo_recv.at[step, side],
                    device_id=device,
                    device_id_type=MESH,
                )
            )
        return out

    halos = [halo(step) for step in range(SUBSTEPS)]
    for copy in halos[0]:
        copy.start()

    lane = iota((npy, LANES), 1)
    tile = ocean[...]
    turn = jnp.concatenate(
        [tile[c, px * PS : (px + 1) * PS] for px in range(2) for c in range(2)] * 2, axis=0
    )
    turned[...] = turn.T
    columns = []
    for j in range(8):
        low = turned[pl.ds(j, npy, stride=PS), :]
        high = turned[pl.ds(8 + j, npy, stride=PS), :]
        columns.append(jnp.where(lane < 64, low, high))
    plain = jnp.concatenate(columns, axis=1)
    swapped = jnp.concatenate([swap_halves(c) for c in columns], axis=1)
    patches = jnp.concatenate([plain, swapped], axis=0)

    src = source_col[...]
    src_row = to_row(src, blocks)
    same = (src == src_row) & (iota((blocks, blocks), 1) < iota((blocks, blocks), 0))
    rank = jnp.sum(same.astype(jnp.int32), axis=1, keepdims=True)
    rank_b[...] = jnp.broadcast_to(rank, (blocks, LANES))
    rank_row = to_row(rank, blocks)
    owner = iota((devices, blocks), 0)
    homes = jnp.concatenate(
        [((src_row == owner) & (rank_row == r)).astype(F32) for r in range(2)], axis=0
    )

    quarter = iota((8, LANES), 0)
    ticks = iota((PS, LANES), 0)

    @pl.loop(0, blocks)
    def _(k):
        def line(ref, row):
            return ref[pl.ds(row, 1), :]

        for pair in range(NB // 2):
            first = line(bond_lanes, NB * k + 2 * pair)
            second = line(bond_lanes, NB * k + 2 * pair + 1)
            start = pl.multiple_of(16 * k + 8 * pair, 8)
            bond_index[pl.ds(start, 8), :] = jnp.where(quarter < 4, first, second)
        four = [line(contact_lanes, NC * k + s) for s in range(NC)]
        index = jnp.where(
            quarter < 4,
            jnp.where(quarter < 2, four[0], four[1]),
            jnp.where(quarter < 6, four[2], four[3]),
        )
        contact_index[pl.ds(pl.multiple_of(8 * k, 8), 8), :] = index
        i, j = line(cell, 2 * k), line(cell, 2 * k + 1)
        fx, fy = line(frac, 2 * k), line(frac, 2 * k + 1)
        col = jnp.where(ticks == i, 1.0 - fx, 0.0) + jnp.where(ticks == i + 1, fx, 0.0)
        row = jnp.where(ticks == j, 1.0 - fy, 0.0) + jnp.where(ticks == j + 1, fy, 0.0)
        at = pl.ds(pl.multiple_of(PS * k, PS), PS)
        col_w[at, :] = col
        row_w[at, :] = row
        high, low = split_bf16(row, 2)
        row_split[pl.ds(pl.multiple_of(2 * PS * k, 2 * PS), 2 * PS), :] = jnp.concatenate(
            [high, low], axis=0
        )

    all_codes().wait_recv()
    asked = codes[...].reshape(devices, LANES)
    match = (asked >= me * 64) & (asked < me * 64 + 64)
    spot = iota((devices, LANES), 1)
    first = jnp.min(jnp.where(match, spot, LANES), axis=1, keepdims=True)
    wish = jnp.where(match, asked - me * 64 + 1, 0)
    ids = [
        jnp.sum(jnp.where(spot == first, wish, 0), axis=1, keepdims=True) - 1,
        jnp.sum(jnp.where(spot == first, 0, wish), axis=1, keepdims=True) - 1,
    ]
    number = iota((devices, npy), 1)
    picks = jnp.concatenate(
        [
            jnp.concatenate(
                [(ids[r] == number + npy * px).astype(F32) for px in (r, 1 - r)], axis=1
            )
            for r in range(2)
        ],
        axis=0,
    )
    served = one_hot_dot(picks, patches, 3)
    wide = half_bit((devices, 8 * LANES)) == 0
    served = jnp.where(wide, served[:devices], served[devices:])
    for j in range(8):
        outgoing[pl.ds(j, devices, stride=8), :] = served[:, j * LANES : (j + 1) * LANES]
    send_blocks(outgoing, incoming, 1)
    id_rows = [to_row(one, devices) for one in ids]
    number = iota((npy, devices), 0)
    takes = jnp.concatenate(
        [
            jnp.concatenate(
                [(id_rows[r] == number + npy * px).astype(F32) for r in (px, 1 - px)], axis=1
            )
            for px in range(2)
        ],
        axis=0,
    )

    def own(step, c):
        return pools[step][pl.ds(PAD + c, blocks, stride=4), :]

    def forces(step):
        pool = pools[step]

        @pl.loop(0, blocks // 4)
        def _(group):
            for inner in range(4):
                k = 4 * group + inner
                for pair in range(NB // 2):
                    p = row_of[NS * k + 2 * pair]
                    q = row_of[NS * k + 2 * pair + 1]
                    low, high = pool[pl.ds(p + PAD, 8), :], pool[pl.ds(q + (PAD - 4), 8), :]
                    table = jnp.where(quarter < 4, low, high)
                    at = pl.ds(pl.multiple_of(16 * k + 8 * pair, 8), 8)
                    bond_got[at, :] = jnp.take_along_axis(
                        table, bond_index[at, :], axis=1, mode="promise_in_bounds"
                    )
                four = [
                    pool[pl.ds(row_of[NS * k + NB + s] + (PAD - 2 * s), 8), :]
                    for s in range(NC)
                ]
                table = jnp.where(
                    quarter < 4,
                    jnp.where(quarter < 2, four[0], four[1]),
                    jnp.where(quarter < 6, four[2], four[3]),
                )
                at = pl.ds(pl.multiple_of(8 * k, 8), 8)
                contact_got[at, :] = jnp.take_along_axis(
                    table, contact_index[at, :], axis=1, mode="promise_in_bounds"
                )

        x, y, u, v = [own(step, c) for c in range(4)]
        total_x = jnp.zeros((blocks, LANES), F32)
        total_y = jnp.zeros((blocks, LANES), F32)
        for s in range(NB):
            got = [bond_got[pl.ds(4 * s + c, blocks, stride=16), :] for c in range(4)]
            stiff = stiff_in[pl.ds(s, blocks, stride=NB), :]
            total_x += stiff * (got[0] - x) + 0.2 * (got[2] - u)
            total_y += stiff * (got[1] - y) + 0.2 * (got[3] - v)
        for s in range(NC):
            dx = contact_got[pl.ds(2 * s, blocks, stride=8), :] - x
            dy = contact_got[pl.ds(2 * s + 1, blocks, stride=8), :] - y
            dist = jnp.sqrt(dx * dx + dy * dy)
            push = 2.0 * jnp.maximum(1.5 - dist, 0.0) / jnp.maximum(dist, 0.5)
            total_x -= push * dx
            total_y -= push * dy
        return total_x, total_y

    def drag_of(step):
        slip_x = current[0] - own(step, 2)
        slip_y = current[1] - own(step, 3)
        half = 0.5 * jnp.sqrt(slip_x * slip_x + slip_y * slip_y)
        return half * slip_x, half * slip_y

    def advance(step, force, drag):
        u = own(step, 2) + 0.05 * (force[0] + drag[0])
        v = own(step, 3) + 0.05 * (force[1] + drag[1])
        x = own(step, 0) + 0.05 * u
        y = own(step, 1) + 0.05 * v
        return x, y, u, v

    def arrive(step):
        for copy in halos[step]:
            copy.wait_recv()

    arrive(0)
    force = forces(0)

    all_blocks(outgoing, incoming, 1).wait_recv()

    @pl.loop(0, blocks // 2)
    def _(group):
        for inner in range(2):
            k = 2 * group + inner
            values = incoming[source_of[k]]
            i = cell[pl.ds(2 * k, 1), :]
            fx = frac[pl.ds(2 * k, 1), :]
            base = jnp.broadcast_to(rank_b[pl.ds(k, 1), :] * 32 + i, (8, LANES))
            for c in range(2):
                total = jnp.zeros((8, LANES), F32)
                for h in range(2):
                    low, high = [
                        jnp.take_along_axis(
                            values, base + (h * 64 + c * 16 + d), axis=1, mode="promise_in_bounds"
                        )
                        for d in range(2)
                    ]
                    weight = row_w[pl.ds(pl.multiple_of(PS * k + 8 * h, 8), 8), :]
                    total += weight * ((1.0 - fx) * low + fx * high)
                current[c, pl.ds(k, 1), :] = jnp.sum(total, axis=0, keepdims=True)

    drag = drag_of(0)
    sum_x, sum_y = drag
    for step in range(SUBSTEPS - 1):
        if step > 0:
            arrive(step)
            force = forces(step)
        for c, value in enumerate(advance(step, force, drag)):
            pools[step + 1][pl.ds(PAD + c, blocks, stride=4), :] = value
        for copy in halos[step + 1]:
            copy.start()
        drag = drag_of(step + 1)
        sum_x, sum_y = sum_x + drag[0], sum_y + drag[1]

    stress[0] = sum_x * (-1.0 / SUBSTEPS)
    stress[1] = sum_y * (-1.0 / SUBSTEPS)
    low_half = iota((8, LANES), 1) < 64

    @pl.loop(0, blocks // 2)
    def _(group):
        for inner in range(2):
            k = 2 * group + inner
            col = col_w[pl.ds(pl.multiple_of(PS * k, PS), PS), :]
            spread = jnp.concatenate(
                [col * stress[0, pl.ds(k, 1), :], col * stress[1, pl.ds(k, 1), :]], axis=0
            )
            high, low = split_bf16(spread, 2)
            right = jnp.concatenate(
                [jnp.concatenate([high] * 4, axis=0), jnp.concatenate([low] * 4, axis=0)], axis=1
            )
            left = row_split[pl.ds(pl.multiple_of(2 * PS * k, 2 * PS), 2 * PS), :]
            left = jnp.concatenate([left, left], axis=1)
            piece = lax.dot_general(
                left, right, (((1,), (1,)), ((), ())), preferred_element_type=F32
            )
            piece = piece[:PS] + piece[PS:]
            pieces[pl.ds(pl.multiple_of(8 * k, 8), 8), :] = jnp.where(
                low_half, piece[:8], piece[8:]
            )

    gathered = jnp.concatenate([pieces[pl.ds(j, blocks, stride=8), :] for j in range(8)], axis=1)
    back = one_hot_dot(homes, gathered, 2)
    back = jnp.where(wide, back[:devices], back[devices:])
    for j in range(8):
        returned[pl.ds(j, devices, stride=8), :] = back[:, j * LANES : (j + 1) * LANES]
    send_blocks(returned, arrived, 2)

    arrive(SUBSTEPS - 1)
    force = forces(SUBSTEPS - 1)
    for c, value in enumerate(advance(SUBSTEPS - 1, force, drag)):
        state_out[pl.ds(c, blocks, stride=4), :] = value

    all_blocks(returned, arrived, 2).wait_recv()
    columns = [arrived[pl.ds(j, devices, stride=8), :] for j in range(8)]
    plain = jnp.concatenate(columns, axis=1)
    swapped = jnp.concatenate([swap_halves(c) for c in columns], axis=1)
    summed = one_hot_dot(takes, jnp.concatenate([plain, swapped], axis=0), 2)
    wide = half_bit((npy, 8 * LANES)) == 0
    summed = jnp.where(wide, summed[:npy], summed[npy:])
    for j in range(8):
        part = summed[:, j * LANES : (j + 1) * LANES]
        turned[pl.ds(j, npy, stride=PS), :] = part
        turned[pl.ds(8 + j, npy, stride=PS), :] = pltpu.roll(part, 64, 1)
    turn = turned[...].T
    for px in range(2):
        for c in range(2):
            start = (px * 2 + c) * PS
            stress_out[c, px * PS : (px + 1) * PS, :] = turn[start : start + PS]

    all_codes().wait_send()
    all_blocks(outgoing, incoming, 1).wait_send()
    all_blocks(returned, arrived, 2).wait_send()
    for step in range(SUBSTEPS):
        for copy in halos[step]:
            copy.wait_send()


def local(
    ocean_current,
    floe_state,
    floe_source,
    floe_patch,
    floe_cell,
    floe_frac,
    bond_blocks,
    bond_lanes,
    bond_stiff,
    contact_blocks,
    contact_lanes,
):
    cols = lax.axis_size("gx")
    rows = lax.axis_size("gy")
    devices = cols * rows
    blocks = floe_state.shape[0]
    region = jnp.concatenate([bond_blocks[:, 0], contact_blocks[:, 0]], axis=1)
    number = jnp.concatenate([bond_blocks[:, 1], contact_blocks[:, 1]], axis=1)
    start = jnp.where(region == 0, 0, blocks + EDGE * (region - 1))
    row_of = (4 * (start + number)).reshape(-1)
    source = floe_source[:, 0]
    code = (source * 64 + floe_patch[:, 0]).reshape(1, blocks)
    code = jnp.pad(code, ((0, 0), (0, LANES - blocks)), constant_values=-1)
    vmem = pl.BlockSpec(memory_space=pltpu.VMEM)
    smem = pl.BlockSpec(memory_space=pltpu.SMEM)
    tile = ocean_current.shape
    pool = pltpu.VMEM((2 * PAD + 4 * (blocks + 4 * EDGE), LANES), F32)
    swap = pltpu.VMEM((8 * devices, LANES), F32)
    state, ocean_stress = pl.pallas_call(
        functools.partial(kernel, cols, rows, blocks),
        out_shape=(
            jax.ShapeDtypeStruct((4 * blocks, LANES), F32),
            jax.ShapeDtypeStruct(tile, F32),
        ),
        in_specs=[smem, smem] + [vmem] * 9,
        out_specs=(vmem, vmem),
        scratch_shapes=[
            pool,
            pool,
            pool,
            pool,
            pltpu.VMEM((devices, 1, LANES), jnp.int32),
            swap,
            pltpu.VMEM((devices, 8, LANES), F32),
            swap,
            swap,
            pltpu.VMEM((tile[2], LANES), F32),
            pltpu.VMEM((16 * blocks, LANES), jnp.int32),
            pltpu.VMEM((8 * blocks, LANES), jnp.int32),
            pltpu.VMEM((16 * blocks, LANES), F32),
            pltpu.VMEM((8 * blocks, LANES), F32),
            pltpu.VMEM((PS * blocks, LANES), F32),
            pltpu.VMEM((PS * blocks, LANES), F32),
            pltpu.VMEM((2 * PS * blocks, LANES), BF16),
            pltpu.VMEM((2, blocks, LANES), F32),
            pltpu.VMEM((blocks, LANES), jnp.int32),
            pltpu.VMEM((8 * blocks, LANES), F32),
            pltpu.VMEM((2, blocks, LANES), F32),
            pltpu.SemaphoreType.DMA((SUBSTEPS, 4)),
            pltpu.SemaphoreType.DMA((SUBSTEPS, 4)),
            pltpu.SemaphoreType.DMA((3,)),
            pltpu.SemaphoreType.DMA((3,)),
        ],
        compiler_params=pltpu.CompilerParams(
            collective_id=0, has_side_effects=True, vmem_limit_bytes=32 * 1024 * 1024
        ),
    )(
        row_of,
        source,
        ocean_current,
        floe_state.reshape(4 * blocks, LANES),
        code,
        floe_source,
        floe_cell.reshape(2 * blocks, LANES),
        floe_frac.reshape(2 * blocks, LANES),
        bond_lanes.reshape(NB * blocks, LANES),
        bond_stiff.reshape(NB * blocks, LANES),
        contact_lanes.reshape(NC * blocks, LANES),
    )
    return (state.reshape(blocks, 4, LANES), ocean_stress)


def solution(mesh):
    whole = P(("gx", "gy"), None, None)
    flat = P(("gx", "gy"), None)
    ocean = P(None, "gx", "gy")
    in_specs = (ocean, whole, flat, flat) + (whole,) * 7
    return jax.shard_map(
        local, mesh=mesh, in_specs=in_specs, out_specs=(whole, ocean), check_vma=False
    )
```

```python
import functools
import jax
import jax.numpy as jnp
from jax import lax
from jax.experimental import pallas as pl
from jax.experimental.pallas import tpu as pltpu
from jax.sharding import PartitionSpec as P

PS = 16
EDGE = 16
NB = 4
NC = 4
NS = NB + NC
SUBSTEPS = 4
LANES = 128
PAD = 8
MESH = pl.DeviceIdType.MESH
F32 = jnp.float32
BF16 = jnp.bfloat16


def iota(shape, dim):
    return lax.broadcasted_iota(jnp.int32, shape, dim)


def split_bf16(value, parts):
    out = []
    for _ in range(parts):
        piece = value.astype(BF16)
        out.append(piece)
        value = value - piece.astype(F32)
    return out


def one_hot_dot(picks, values, parts):
    left = picks.astype(BF16)
    left = jnp.concatenate([left] * parts, axis=1)
    right = jnp.concatenate(split_bf16(values, parts), axis=0)
    return jnp.dot(left, right, preferred_element_type=F32)


def half_bit(shape):
    return (iota(shape, 1) // 32) % 2


def swap_halves(value):
    ahead = pltpu.roll(value, LANES - 32, 1)
    behind = pltpu.roll(value, 32, 1)
    return jnp.where(half_bit(value.shape) == 0, ahead, behind)


def to_row(column, count):
    eye = iota((count, count), 0) == iota((count, count), 1)
    return jnp.sum(jnp.where(eye, column, 0), axis=0, keepdims=True)


def to_column(row, count):
    eye = iota((count, count), 0) == iota((count, count), 1)
    return jnp.sum(jnp.where(eye, row, 0), axis=1, keepdims=True)


def kernel(
    cols,
    rows,
    blocks,
    bond_blocks,
    contact_blocks,
    source_of,
    source_row,
    patch_row,
    state_far,
    ocean_far,
    cell_far,
    frac_far,
    bond_far,
    contact_far,
    stiff_far,
    state_out,
    stress_out,
    ocean,
    cell,
    frac,
    bond_lanes,
    contact_lanes,
    stiff_in,
    row_of,
    fetch_sem,
    patches,
    state_near,
    stress_near,
    store_sem,
    pool0,
    pool1,
    pool2,
    pool3,
    codes,
    outgoing,
    incoming,
    returned,
    arrived,
    turned,
    bond_index,
    contact_index,
    bond_got,
    contact_got,
    row_w,
    col_w,
    row_split,
    current,
    rank_b,
    pieces,
    stress,
    halo_send,
    halo_recv,
    all_send,
    all_recv,
):
    pools = (pool0, pool1, pool2, pool3)
    devices = cols * rows
    ax = lax.axis_index("gx")
    by = lax.axis_index("gy")
    me = ax * rows + by
    npy = ocean.shape[2] // PS

    own_state = pl.ds(PAD, 4 * blocks)
    fetches = [
        pltpu.make_async_copy(far, near, fetch_sem.at[n])
        for n, (far, near) in enumerate(
            (
                (state_far, pool0.at[own_state, :]),
                (ocean_far, ocean),
                (bond_far, bond_lanes),
                (contact_far, contact_lanes),
                (cell_far, cell),
                (frac_far, frac),
                (stiff_far, stiff_in),
            )
        )
    ]
    for copy in fetches:
        copy.start()

    def wrap(value, size):
        return jnp.where(value >= size, value - size, value)

    to_a = [wrap(ax + i, cols) for i in range(cols)]
    to_b = [wrap(by + j, rows) for j in range(rows)]
    others = [(to_a[i], to_b[j]) for i in range(cols) for j in range(rows) if i or j]

    barrier = pltpu.get_barrier_semaphore()
    for device in others:
        pl.semaphore_signal(barrier, inc=1, device_id=device, device_id_type=MESH)

    src_row = source_row[...]
    code = jnp.full((1, LANES - blocks), -1, jnp.int32)
    code = jnp.concatenate([src_row * 64 + patch_row[...], code], axis=1)
    codes[pl.ds(me, 1)] = code.reshape(1, 1, LANES)
    for pool in pools:
        pool[pl.ds(0, PAD), :] = jnp.zeros((PAD, LANES), F32)
        pool[pl.ds(PAD + 4 * (blocks + 4 * EDGE), PAD), :] = jnp.zeros((PAD, LANES), F32)
    pl.semaphore_wait(barrier, devices - 1)

    def all_copy(source, target, which, device):
        return pltpu.make_async_remote_copy(
            src_ref=source,
            dst_ref=target,
            send_sem=all_send.at[which],
            recv_sem=all_recv.at[which],
            device_id=device,
            device_id_type=MESH,
        )

    other = others[0]

    for device in others:
        all_copy(codes.at[pl.ds(me, 1)], codes.at[pl.ds(me, 1)], 0, device).start()

    def all_codes():
        part = codes.at[pl.ds(0, devices - 1)]
        return all_copy(part, part, 0, other)

    def all_blocks(outs, ins, which):
        size = 8 * (devices - 1)
        return all_copy(outs.at[pl.ds(0, size), :], outs.at[pl.ds(0, size), :], which, other)

    def send_blocks(outs, ins, which):
        mine = pl.ds(pl.multiple_of(me * 8, 8), 8)
        land = ins.at[me] if which == 1 else ins.at[mine, :]

        for device in others:
            to = device[0] * rows + device[1]
            part = outs.at[pl.ds(pl.multiple_of(to * 8, 8), 8), :]
            all_copy(part, land, which, device).start()

        land[...] = outs[mine, :]

    last = PAD + 4 * (blocks - EDGE)
    targets = (
        (last, (to_a[1], by)),
        (PAD, (to_a[-1], by)),
        (last, (ax, to_b[1])),
        (PAD, (ax, to_b[-1])),
    )

    def halo(step):
        pool = pools[step]
        out = []
        for side, (start, device) in enumerate(targets):
            out.append(
                pltpu.make_async_remote_copy(
                    src_ref=pool.at[pl.ds(start, 4 * EDGE), :],
                    dst_ref=pool.at[pl.ds(PAD + 4 * (blocks + side * EDGE), 4 * EDGE), :],
                    send_sem=halo_send.at[step, side],
                    recv_sem=halo_recv.at[step, side],
                    device_id=device,
                    device_id_type=MESH,
                )
            )
        return out

    halos = [halo(step) for step in range(SUBSTEPS)]
    fetches[0].wait()
    for copy in halos[0]:
        copy.start()

    for copy in fetches[1:]:
        copy.wait()
    lane = iota((npy, LANES), 1)
    tile = ocean[...]
    turn = jnp.concatenate(
        [tile[c, px * PS : (px + 1) * PS] for px in range(2) for c in range(2)] * 2, axis=0
    )
    turned[...] = turn.T
    columns = []
    for j in range(8):
        low = turned[pl.ds(j, npy, stride=PS), :]
        high = turned[pl.ds(8 + j, npy, stride=PS), :]
        columns.append(jnp.where(lane < 64, low, high))
    plain = jnp.concatenate(columns, axis=1)
    swapped = jnp.concatenate([swap_halves(c) for c in columns], axis=1)
    patches[...] = jnp.concatenate(
        split_bf16(jnp.concatenate([plain, swapped], axis=0), 3), axis=0
    )

    src = to_column(src_row, blocks)
    same = (src == src_row) & (iota((blocks, blocks), 1) < iota((blocks, blocks), 0))
    rank = jnp.sum(same.astype(jnp.int32), axis=1, keepdims=True)
    rank_b[...] = jnp.broadcast_to(rank, (blocks, LANES))
    rank_row = to_row(rank, blocks)
    owner = iota((devices, blocks), 0)
    homes = jnp.concatenate(
        [((src_row == owner) & (rank_row == r)).astype(F32) for r in range(2)], axis=0
    )

    quarter = iota((8, LANES), 0)
    ticks = iota((PS, LANES), 0)

    @pl.loop(0, blocks)
    def _(k):
        for s in range(NS):
            table = bond_blocks if s < NB else contact_blocks
            region = table[0, s % NB, k]
            start = jnp.where(region == 0, 0, blocks + EDGE * (region - 1))
            row_of[NS * k + s] = 4 * (start + table[1, s % NB, k])

        def line(ref, row):
            return ref[pl.ds(row, 1), :]

        for pair in range(NB // 2):
            first = line(bond_lanes, NB * k + 2 * pair)
            second = line(bond_lanes, NB * k + 2 * pair + 1)
            start = pl.multiple_of(16 * k + 8 * pair, 8)
            bond_index[pl.ds(start, 8), :] = jnp.where(quarter < 4, first, second)
        four = [line(contact_lanes, NC * k + s) for s in range(NC)]
        index = jnp.where(
            quarter < 4,
            jnp.where(quarter < 2, four[0], four[1]),
            jnp.where(quarter < 6, four[2], four[3]),
        )
        contact_index[pl.ds(pl.multiple_of(8 * k, 8), 8), :] = index
        i, j = line(cell, 2 * k), line(cell, 2 * k + 1)
        fx, fy = line(frac, 2 * k), line(frac, 2 * k + 1)
        col = jnp.where(ticks == i, 1.0 - fx, 0.0) + jnp.where(ticks == i + 1, fx, 0.0)
        row = jnp.where(ticks == j, 1.0 - fy, 0.0) + jnp.where(ticks == j + 1, fy, 0.0)
        at = pl.ds(pl.multiple_of(PS * k, PS), PS)
        col_w[at, :] = col
        row_w[at, :] = row
        high, low = split_bf16(row, 2)
        row_split[pl.ds(pl.multiple_of(2 * PS * k, 2 * PS), 2 * PS), :] = jnp.concatenate(
            [high, low], axis=0
        )

    all_codes().wait_recv()
    asked = codes[...].reshape(devices, LANES)
    match = (asked >= me * 64) & (asked < me * 64 + 64)
    spot = iota((devices, LANES), 1)
    first = jnp.min(jnp.where(match, spot, LANES), axis=1, keepdims=True)
    wish = jnp.where(match, asked - me * 64 + 1, 0)
    ids = [
        jnp.sum(jnp.where(spot == first, wish, 0), axis=1, keepdims=True) - 1,
        jnp.sum(jnp.where(spot == first, 0, wish), axis=1, keepdims=True) - 1,
    ]
    number = iota((devices, npy), 1)
    picks = jnp.concatenate(
        [
            jnp.concatenate(
                [(ids[r] == number + npy * px).astype(F32) for px in (r, 1 - r)], axis=1
            )
            for r in range(2)
        ],
        axis=0,
    )
    picks = jnp.concatenate([picks.astype(BF16)] * 3, axis=1)
    served = jnp.dot(picks, patches[...], preferred_element_type=F32)
    wide = half_bit((devices, 8 * LANES)) == 0
    served = jnp.where(wide, served[:devices], served[devices:])
    for j in range(8):
        outgoing[pl.ds(j, devices, stride=8), :] = served[:, j * LANES : (j + 1) * LANES]
    send_blocks(outgoing, incoming, 1)
    id_rows = [to_row(one, devices) for one in ids]
    number = iota((npy, devices), 0)
    takes = jnp.concatenate(
        [
            jnp.concatenate(
                [(id_rows[r] == number + npy * px).astype(F32) for r in (px, 1 - px)], axis=1
            )
            for px in range(2)
        ],
        axis=0,
    )

    def own(step, c):
        return pools[step][pl.ds(PAD + c, blocks, stride=4), :]

    def forces(step):
        pool = pools[step]

        @pl.loop(0, blocks // 8)
        def _(group):
            for inner in range(8):
                k = 8 * group + inner
                for pair in range(NB // 2):
                    p = row_of[NS * k + 2 * pair]
                    q = row_of[NS * k + 2 * pair + 1]
                    low, high = pool[pl.ds(p + PAD, 8), :], pool[pl.ds(q + (PAD - 4), 8), :]
                    table = jnp.where(quarter < 4, low, high)
                    at = pl.ds(pl.multiple_of(16 * k + 8 * pair, 8), 8)
                    bond_got[at, :] = jnp.take_along_axis(
                        table, bond_index[at, :], axis=1, mode="promise_in_bounds"
                    )
                four = [
                    pool[pl.ds(row_of[NS * k + NB + s] + (PAD - 2 * s), 8), :]
                    for s in range(NC)
                ]
                table = jnp.where(
                    quarter < 4,
                    jnp.where(quarter < 2, four[0], four[1]),
                    jnp.where(quarter < 6, four[2], four[3]),
                )
                at = pl.ds(pl.multiple_of(8 * k, 8), 8)
                contact_got[at, :] = jnp.take_along_axis(
                    table, contact_index[at, :], axis=1, mode="promise_in_bounds"
                )

        x, y, u, v = [own(step, c) for c in range(4)]
        total_x = jnp.zeros((blocks, LANES), F32)
        total_y = jnp.zeros((blocks, LANES), F32)
        for s in range(NB):
            got = [bond_got[pl.ds(4 * s + c, blocks, stride=16), :] for c in range(4)]
            stiff = stiff_in[pl.ds(s, blocks, stride=NB), :]
            total_x += stiff * (got[0] - x) + 0.2 * (got[2] - u)
            total_y += stiff * (got[1] - y) + 0.2 * (got[3] - v)
        for s in range(NC):
            dx = contact_got[pl.ds(2 * s, blocks, stride=8), :] - x
            dy = contact_got[pl.ds(2 * s + 1, blocks, stride=8), :] - y
            dist = jnp.sqrt(dx * dx + dy * dy)
            push = 2.0 * jnp.maximum(1.5 - dist, 0.0) / jnp.maximum(dist, 0.5)
            total_x -= push * dx
            total_y -= push * dy
        return total_x, total_y

    def drag_of(step):
        slip_x = current[0] - own(step, 2)
        slip_y = current[1] - own(step, 3)
        half = 0.5 * jnp.sqrt(slip_x * slip_x + slip_y * slip_y)
        return half * slip_x, half * slip_y

    def advance(step, force, drag):
        u = own(step, 2) + 0.05 * (force[0] + drag[0])
        v = own(step, 3) + 0.05 * (force[1] + drag[1])
        x = own(step, 0) + 0.05 * u
        y = own(step, 1) + 0.05 * v
        return x, y, u, v

    def arrive(step):
        for copy in halos[step]:
            copy.wait_recv()

    arrive(0)
    force = forces(0)

    all_blocks(outgoing, incoming, 1).wait_recv()

    @pl.loop(0, blocks // 8)
    def _(group):
        for inner in range(8):
            k = 8 * group + inner
            values = incoming[source_of[0, k]]
            i = cell[pl.ds(2 * k, 1), :]
            fx = frac[pl.ds(2 * k, 1), :]
            base = jnp.broadcast_to(rank_b[pl.ds(k, 1), :] * 32 + i, (8, LANES))
            for c in range(2):
                total = jnp.zeros((8, LANES), F32)
                for h in range(2):
                    low, high = [
                        jnp.take_along_axis(
                            values, base + (h * 64 + c * 16 + d), axis=1, mode="promise_in_bounds"
                        )
                        for d in range(2)
                    ]
                    weight = row_w[pl.ds(pl.multiple_of(PS * k + 8 * h, 8), 8), :]
                    total += weight * ((1.0 - fx) * low + fx * high)
                current[c, pl.ds(k, 1), :] = jnp.sum(total, axis=0, keepdims=True)

    drag = drag_of(0)
    sum_x, sum_y = drag
    for step in range(SUBSTEPS - 1):
        if step > 0:
            arrive(step)
            force = forces(step)
        for c, value in enumerate(advance(step, force, drag)):
            pools[step + 1][pl.ds(PAD + c, blocks, stride=4), :] = value
        for copy in halos[step + 1]:
            copy.start()
        drag = drag_of(step + 1)
        sum_x, sum_y = sum_x + drag[0], sum_y + drag[1]

    stress[0] = sum_x * (-1.0 / SUBSTEPS)
    stress[1] = sum_y * (-1.0 / SUBSTEPS)
    low_half = iota((8, LANES), 1) < 64

    @pl.loop(0, blocks // 8)
    def _(group):
        for inner in range(8):
            k = 8 * group + inner
            col = col_w[pl.ds(pl.multiple_of(PS * k, PS), PS), :]
            spread = jnp.concatenate(
                [col * stress[0, pl.ds(k, 1), :], col * stress[1, pl.ds(k, 1), :]], axis=0
            )
            high, low = split_bf16(spread, 2)
            right = jnp.concatenate(
                [jnp.concatenate([high] * 4, axis=0), jnp.concatenate([low] * 4, axis=0)], axis=1
            )
            left = row_split[pl.ds(pl.multiple_of(2 * PS * k, 2 * PS), 2 * PS), :]
            left = jnp.concatenate([left, left], axis=1)
            piece = lax.dot_general(
                left, right, (((1,), (1,)), ((), ())), preferred_element_type=F32
            )
            piece = piece[:PS] + piece[PS:]
            pieces[pl.ds(pl.multiple_of(8 * k, 8), 8), :] = jnp.where(
                low_half, piece[:8], piece[8:]
            )

    gathered = jnp.concatenate([pieces[pl.ds(j, blocks, stride=8), :] for j in range(8)], axis=1)
    back = one_hot_dot(homes, gathered, 2)
    back = jnp.where(wide, back[:devices], back[devices:])
    for j in range(8):
        returned[pl.ds(j, devices, stride=8), :] = back[:, j * LANES : (j + 1) * LANES]
    send_blocks(returned, arrived, 2)

    arrive(SUBSTEPS - 1)
    force = forces(SUBSTEPS - 1)
    for c, value in enumerate(advance(SUBSTEPS - 1, force, drag)):
        state_near[pl.ds(c, blocks, stride=4), :] = value
    store_state = pltpu.make_async_copy(state_near, state_out, store_sem.at[0])
    store_state.start()

    all_blocks(returned, arrived, 2).wait_recv()
    columns = [arrived[pl.ds(j, devices, stride=8), :] for j in range(8)]
    plain = jnp.concatenate(columns, axis=1)
    swapped = jnp.concatenate([swap_halves(c) for c in columns], axis=1)
    summed = one_hot_dot(takes, jnp.concatenate([plain, swapped], axis=0), 2)
    wide = half_bit((npy, 8 * LANES)) == 0
    summed = jnp.where(wide, summed[:npy], summed[npy:])
    for j in range(8):
        part = summed[:, j * LANES : (j + 1) * LANES]
        turned[pl.ds(j, npy, stride=PS), :] = part
        turned[pl.ds(8 + j, npy, stride=PS), :] = pltpu.roll(part, 64, 1)
    turn = turned[...].T
    for px in range(2):
        for c in range(2):
            start = (px * 2 + c) * PS
            stress_near[c, px * PS : (px + 1) * PS, :] = turn[start : start + PS]
    store_stress = pltpu.make_async_copy(stress_near, stress_out, store_sem.at[1])
    store_stress.start()

    all_codes().wait_send()
    all_blocks(outgoing, incoming, 1).wait_send()
    all_blocks(returned, arrived, 2).wait_send()
    for step in range(SUBSTEPS):
        for copy in halos[step]:
            copy.wait_send()
    store_state.wait()
    store_stress.wait()


def local(
    ocean_current,
    floe_state,
    floe_source,
    floe_patch,
    floe_cell,
    floe_frac,
    bond_blocks,
    bond_lanes,
    bond_stiff,
    contact_blocks,
    contact_lanes,
):
    cols = lax.axis_size("gx")
    rows = lax.axis_size("gy")
    devices = cols * rows
    blocks = floe_state.shape[0]
    vmem = pl.BlockSpec(memory_space=pltpu.VMEM)
    smem = pl.BlockSpec(memory_space=pltpu.SMEM)
    far = pl.BlockSpec(memory_space=pltpu.HBM)
    tile = ocean_current.shape
    ints = jnp.int32
    pool = pltpu.VMEM((2 * PAD + 4 * (blocks + 4 * EDGE), LANES), F32)
    swap = pltpu.VMEM((8 * devices, LANES), F32)
    state, ocean_stress = pl.pallas_call(
        functools.partial(kernel, cols, rows, blocks),
        out_shape=(
            jax.ShapeDtypeStruct((4 * blocks, LANES), F32),
            jax.ShapeDtypeStruct(tile, F32),
        ),
        in_specs=[smem] * 3 + [vmem] * 2 + [far] * 7,
        out_specs=(far, far),
        scratch_shapes=[
            pltpu.VMEM(tile, F32),
            pltpu.VMEM((2 * blocks, LANES), ints),
            pltpu.VMEM((2 * blocks, LANES), F32),
            pltpu.VMEM((NB * blocks, LANES), ints),
            pltpu.VMEM((NC * blocks, LANES), ints),
            pltpu.VMEM((NB * blocks, LANES), F32),
            pltpu.SMEM((NS * blocks,), ints),
            pltpu.SemaphoreType.DMA((7,)),
            pltpu.VMEM((6 * (tile[2] // PS), 8 * LANES), BF16),
            pltpu.VMEM((4 * blocks, LANES), F32),
            pltpu.VMEM(tile, F32),
            pltpu.SemaphoreType.DMA((2,)),
            pool,
            pool,
            pool,
            pool,
            pltpu.VMEM((devices, 1, LANES), jnp.int32),
            swap,
            pltpu.VMEM((devices, 8, LANES), F32),
            swap,
            swap,
            pltpu.VMEM((tile[2], LANES), F32),
            pltpu.VMEM((16 * blocks, LANES), jnp.int32),
            pltpu.VMEM((8 * blocks, LANES), jnp.int32),
            pltpu.VMEM((16 * blocks, LANES), F32),
            pltpu.VMEM((8 * blocks, LANES), F32),
            pltpu.VMEM((PS * blocks, LANES), F32),
            pltpu.VMEM((PS * blocks, LANES), F32),
            pltpu.VMEM((2 * PS * blocks, LANES), BF16),
            pltpu.VMEM((2, blocks, LANES), F32),
            pltpu.VMEM((blocks, LANES), jnp.int32),
            pltpu.VMEM((8 * blocks, LANES), F32),
            pltpu.VMEM((2, blocks, LANES), F32),
            pltpu.SemaphoreType.DMA((SUBSTEPS, 4)),
            pltpu.SemaphoreType.DMA((SUBSTEPS, 4)),
            pltpu.SemaphoreType.DMA((3,)),
            pltpu.SemaphoreType.DMA((3,)),
        ],
        compiler_params=pltpu.CompilerParams(
            collective_id=0, has_side_effects=True, vmem_limit_bytes=63 * 1024 * 1024
        ),
    )(
        bond_blocks.transpose(1, 2, 0),
        contact_blocks.transpose(1, 2, 0),
        floe_source.T,
        floe_source.T,
        floe_patch.T,
        floe_state.reshape(4 * blocks, LANES),
        ocean_current,
        floe_cell.reshape(2 * blocks, LANES),
        floe_frac.reshape(2 * blocks, LANES),
        bond_lanes.reshape(NB * blocks, LANES),
        contact_lanes.reshape(NC * blocks, LANES),
        bond_stiff.reshape(NB * blocks, LANES),
    )
    return (state.reshape(blocks, 4, LANES), ocean_stress)


def solution(mesh):
    whole = P(("gx", "gy"), None, None)
    flat = P(("gx", "gy"), None)
    ocean = P(None, "gx", "gy")
    in_specs = (ocean, whole, flat, flat) + (whole,) * 7
    return jax.shard_map(
        local, mesh=mesh, in_specs=in_specs, out_specs=(whole, ocean), check_vma=False
    )
```
